32 devices in a mesh: section: 2 (over y), expert: 16 (over z, x, core).
Axes of the slice: x: 2, y: 2, z: 4, core: 2. Of those that a mesh axis runs over, the one named last changes fastest.
Arguments:
- x_forward: bfloat16 [2, 1024, 1024], P('section', 'expert'), may hold values from -6 to 6
- route_forward: int32 [2, 1024, 8], P('section', 'expert'), may hold values from 0 to 15, all different within a row; in each aligned block of 64 rows (0 to 63, 64 to 127, ..., all dimensions but the last counted through in order) at most 36 rows name the same one
- gate_forward: float32 [2, 1024, 8], P('section', 'expert'), may hold values from 0.05 to 0.6
- x_backward: bfloat16 [2, 1024, 1024], P('section', 'expert'), may hold values from -6 to 6
- route_backward: int32 [2, 1024, 8], P('section', 'expert'), may hold values from 0 to 15, all different within a row; in each aligned block of 64 rows (0 to 63, 64 to 127, ..., all dimensions but the last counted through in order) at most 36 rows name the same one
- gate_backward: float32 [2, 1024, 8], P('section', 'expert'), may hold values from 0.05 to 0.6
- cotangent: bfloat16 [2, 1024, 1024], P('section', 'expert'), may hold values from -6 to 6
- w_gate: bfloat16 [2, 16, 1024, 384], P('section', 'expert'), may hold values from -0.1875 to 0.1875
- w_up: bfloat16 [2, 16, 1024, 384], P('section', 'expert'), may hold values from -0.1875 to 0.1875
- w_down: bfloat16 [2, 16, 384, 1024], P('section', 'expert'), may hold values from -0.3125 to 0.3125
Outputs:
- arrived_forward: bfloat16 [2, 1024, 1024], P('section', 'expert')
- arrived_backward: bfloat16 [2, 1024, 1024], P('section', 'expert')
The draws below stay inside these ranges and needn't reach their ends.
Inputs may be any that keep to these rules, and one draw needn't show every extreme that they name: `route_forward`: each token names 8 different experts. Among the 64 tokens of one aligned block no expert is named more than 36 times, a bound that some block reaches; every expert is named somewhere. `route_backward`: as for route_forward.
All inputs are finite; a program needn't handle non-finite values.
Results may differ from the reference program's by a relative error of at most 0.0049.
Values may be sent and summed in bfloat16 or wider, within the bound.
No kernel may reach another device: no remote copies, remote signals or barrier semaphores. Data moves between devices by JAX's collectives and lax.ppermute only.
A program may use at most 64 MiB of HBM per device.

```python
import math
import jax
import jax.numpy as jnp
import numpy as np
from jax import lax

D = 1024
FFE = 384
TOPK = 8
TOK_DEV = 64
EXPERTS = 16
CAP = 36
TOKENS = 1024
N_SECTION = 2
N_EXPERT = 16


def levels(own_key, dims, cuts, smallest, largest):
    factor_of = 1.0
    for position, parts in cuts:
        steps = jax.random.uniform(jax.random.fold_in(jax.random.fold_in(own_key, 6), position), (parts,), jnp.float32, smallest / len(cuts), largest / len(cuts))
        factor_of = factor_of * jnp.repeat(jnp.exp(steps), dims[position] // parts).reshape((-1,) + (1,) * (len(dims) - 1 - position))
    return factor_of


def deal_out(own_key, own, number, rows, amount, top, limit, skew):
    ranking = jax.random.permutation(own_key, amount)
    crowded, ordinary = shares(amount, rows * top, limit, skew, True), shares(amount, rows * top, limit, skew, False)
    places = jnp.arange(amount)

    def named(tallies, rotation):
        used = int((tallies > 0).sum())
        fixed = max(1, used // 4)
        shifted = fixed + (places - fixed + rotation * (used - fixed)) % max(1, amount - fixed)
        return jnp.zeros((amount,), jnp.int32).at[ranking[jnp.where(places < fixed, places, shifted)]].set(jnp.asarray(tallies, jnp.int32))

    tallies = jnp.where(number % 4 == 0, named(crowded, number // 4), named(ordinary, number - number // 4 - 1))
    mixed = jax.random.permutation(jax.random.fold_in(own, 3), amount)
    giver, taker = mixed[0:amount // 2 * 2:2], mixed[1:amount // 2 * 2:2]
    slack = jnp.minimum(tallies[giver] - 1, limit - tallies[taker]) // 2
    slack = jnp.where((giver == ranking[0]) | (taker == ranking[0]) | (tallies[taker] == 0), 0, jnp.maximum(slack, 0))
    shifted = jax.random.randint(jax.random.fold_in(own, 4), (amount // 2,), 0, 1 << 20) % (slack + 1)
    tallies = tallies.at[giver].add(-shifted).at[taker].add(shifted)
    items = jnp.searchsorted(jnp.cumsum(tallies), jnp.arange(rows * top), side="right").astype(jnp.int32)
    grid = items.reshape(top, rows).T
    grid = grid[jax.random.permutation(jax.random.fold_in(own, 1), rows)]
    rotation = jax.random.randint(jax.random.fold_in(own, 2), (rows, 1), 0, top)
    return jnp.take_along_axis(grid, (jnp.arange(top)[None, :] + rotation) % top, axis=1)


def shares(count, total, most, lean, full):
    weights = [(1 << 20) // math.isqrt(rank ** lean) + 1 for rank in range(1, count + 1)]
    largest = most if full else min(most, max(-(-total // count), total * weights[0] // sum(weights)))
    least = 1 if total - largest >= count - 1 else 0
    holding, surplus = [largest] + [least] * (count - 1), total - largest - least * (count - 1)
    while surplus > 0:
        free = [i for i in range(1, count) if holding[i] < largest] or [i for i in range(1, count) if holding[i] < most]
        whole, left = sum([weights[i] for i in free]), surplus
        for i in free:
            more = min(most - holding[i], max(1, left * weights[i] // whole), surplus)
            holding[i] = holding[i] + more
            surplus = surplus - more
    return np.array(holding)


def normal_values(stream_key, shape, scale, most, pieces=(), kind=jnp.bfloat16):
    entries = scale * jax.random.normal(stream_key, shape, jnp.float32)
    if pieces:
        entries = entries * levels(stream_key, shape, pieces, -0.22, 0.18)
    return jnp.clip(entries, -most, most).astype(kind)


def setup_inputs(seed: int = 0) -> dict:
    keys = jax.random.split(jax.random.key(seed), 11)
    x_forward = normal_values(keys[0], (N_SECTION, TOKENS, D), 1.0, 6.0, ((0, 2), (1, 16)))
    route_forward_keys = jax.random.split(jax.random.fold_in(keys[1], 1), N_SECTION * TOKENS // TOK_DEV)
    route_forward_turns = jax.random.permutation(jax.random.fold_in(keys[1], 3), N_SECTION * TOKENS // TOK_DEV)
    route_forward = jax.vmap(lambda own, number: deal_out(jax.random.fold_in(keys[1], 2), own, number, TOK_DEV, EXPERTS, TOPK, CAP, 2))(route_forward_keys, route_forward_turns).reshape((N_SECTION, TOKENS, TOPK))
    gate_forward = jnp.clip(0.05 + 0.55 * jax.random.uniform(keys[2], (N_SECTION, TOKENS, TOPK), jnp.float32) ** levels(keys[2], (N_SECTION, TOKENS, TOPK), ((0, 2), (1, 16)), -0.2, 0.2), 0.05, 0.6)
    x_backward = normal_values(keys[3], (N_SECTION, TOKENS, D), 1.0, 6.0, ((0, 2), (1, 16)))
    route_backward_keys = jax.random.split(jax.random.fold_in(keys[4], 1), N_SECTION * TOKENS // TOK_DEV)
    route_backward_turns = jax.random.permutation(jax.random.fold_in(keys[4], 3), N_SECTION * TOKENS // TOK_DEV)
    route_backward = jax.vmap(lambda own, number: deal_out(jax.random.fold_in(keys[4], 2), own, number, TOK_DEV, EXPERTS, TOPK, CAP, 2))(route_backward_keys, route_backward_turns).reshape((N_SECTION, TOKENS, TOPK))
    gate_backward = jnp.clip(0.05 + 0.55 * jax.random.uniform(keys[5], (N_SECTION, TOKENS, TOPK), jnp.float32) ** levels(keys[5], (N_SECTION, TOKENS, TOPK), ((0, 2), (1, 16)), -0.2, 0.2), 0.05, 0.6)
    cotangent = normal_values(keys[6], (N_SECTION, TOKENS, D), 1.0, 6.0, ((0, 2), (1, 16)))
    w_gate = normal_values(keys[7], (N_SECTION, EXPERTS, D, FFE), D ** -0.5, 0.1875, ((0, 2), (1, 16)))
    w_up = normal_values(keys[8], (N_SECTION, EXPERTS, D, FFE), D ** -0.5, 0.1875, ((0, 2), (1, 16)))
    w_down = normal_values(keys[9], (N_SECTION, EXPERTS, FFE, D), FFE ** -0.5, 0.3125, ((0, 2), (1, 16)))
    return {"x_forward": x_forward, "route_forward": route_forward, "gate_forward": gate_forward, "x_backward": x_backward, "route_backward": route_backward, "gate_backward": gate_backward, "cotangent": cotangent, "w_gate": w_gate, "w_up": w_up, "w_down": w_down}


def slot_order(route):
    flat_ids = route.reshape(-1, TOK_DEV * TOPK)
    one_hot = (flat_ids[:, :, None] == jnp.arange(EXPERTS, dtype=jnp.int32)[None, None, :]).astype(jnp.int32)
    before = jnp.cumsum(one_hot, axis=1) - one_hot
    rank = jnp.sum(before * one_hot, axis=2)
    block_ids = jnp.arange(flat_ids.shape[0], dtype=jnp.int32)[:, None]
    flat = flat_ids * (N_EXPERT * CAP) + block_ids * CAP + rank
    return flat.reshape(-1).astype(jnp.int32)


def expert_forward(rows, gate_mat, up_mat, down_mat):
    pre_gate = jnp.dot(rows, gate_mat, preferred_element_type=jnp.float32)
    pre_up = jnp.dot(rows, up_mat, preferred_element_type=jnp.float32)
    hidden = (pre_gate * jax.nn.sigmoid(pre_gate) * pre_up).astype(jnp.bfloat16)
    return jnp.dot(hidden, down_mat, preferred_element_type=jnp.float32).astype(jnp.bfloat16)


def expert_backward(rows, cots, gate_mat, up_mat, down_mat):
    pre_gate = jnp.dot(rows, gate_mat, preferred_element_type=jnp.float32)
    pre_up = jnp.dot(rows, up_mat, preferred_element_type=jnp.float32)
    sig_gate = jax.nn.sigmoid(pre_gate)
    d_hidden = jnp.dot(cots, down_mat.T, preferred_element_type=jnp.float32)
    d_gate = (d_hidden * pre_up * sig_gate * (1.0 + pre_gate * (1.0 - sig_gate))).astype(jnp.bfloat16)
    d_up = (d_hidden * pre_gate * sig_gate).astype(jnp.bfloat16)
    total = jnp.dot(d_gate, gate_mat.T, preferred_element_type=jnp.float32)
    total = total + jnp.dot(d_up, up_mat.T, preferred_element_type=jnp.float32)
    return total.astype(jnp.bfloat16)


def place(rows, slots):
    buffer = jnp.zeros((EXPERTS * N_EXPERT * CAP, rows.shape[1]), rows.dtype)
    return buffer.at[slots].set(rows).reshape(EXPERTS, N_EXPERT * CAP, rows.shape[1])


def one_section(items):
    x_fwd, r_fwd, g_fwd, x_bwd, r_bwd, g_bwd, cots, gate_all, up_all, down_all = items
    slots_fwd = slot_order(r_fwd)
    placed = place(jnp.repeat(x_fwd, TOPK, axis=0), slots_fwd)
    outs = lax.map(lambda piece: expert_forward(piece[0], piece[1], piece[2], piece[3]), (placed, gate_all, up_all, down_all))
    picked = outs.reshape(-1, D)[slots_fwd].reshape(TOKENS, TOPK, D).astype(jnp.float32)
    layer_out = x_fwd.astype(jnp.float32) + jnp.einsum("tk,tkd->td", g_fwd, picked, precision=lax.Precision.HIGHEST)
    slots_bwd = slot_order(r_bwd)
    placed_x = place(jnp.repeat(x_bwd, TOPK, axis=0), slots_bwd)
    placed_c = place(jnp.repeat(cots, TOPK, axis=0), slots_bwd)
    grads = lax.map(lambda piece: expert_backward(piece[0], piece[1], piece[2], piece[3], piece[4]), (placed_x, placed_c, gate_all, up_all, down_all))
    picked_b = grads.reshape(-1, D)[slots_bwd].reshape(TOKENS, TOPK, D).astype(jnp.float32)
    input_grad = cots.astype(jnp.float32) + jnp.einsum("tk,tkd->td", g_bwd, picked_b, precision=lax.Precision.HIGHEST)
    return layer_out.astype(jnp.bfloat16), input_grad.astype(jnp.bfloat16)


def reference(x_forward, route_forward, gate_forward, x_backward, route_backward, gate_backward, cotangent, w_gate, w_up, w_down):
    layer_out, input_grad = lax.map(one_section, (x_forward, route_forward, gate_forward, x_backward, route_backward, gate_backward, cotangent, w_gate, w_up, w_down))
    return jnp.roll(layer_out, 1, axis=0), jnp.roll(input_grad, -1, axis=0)
```

```python
import functools

import jax
import jax.numpy as jnp
from jax import lax
from jax.experimental import pallas as pl
from jax.experimental.pallas import tpu as pltpu
from jax.sharding import PartitionSpec as P

F32 = jnp.float32
BF16 = jnp.bfloat16
LANES = 128
VMEM_LIMIT = 48 * 1024 * 1024


def passed_along(block, axis, distance):
    devices = range(lax.axis_size(axis))
    route = [((i - distance) % len(devices), i) for i in devices]
    return lax.ppermute(block, axis, route)


def swapped(block, bit):
    return lax.ppermute(block, "expert", [(i, i ^ bit) for i in range(lax.axis_size("expert"))])


def spread(block, bits):
    held, order = block, [0]
    for bit in bits[:-1]:
        held = jnp.concatenate([held, swapped(held, bit)], axis=0)
        order = order + [r | bit for r in order]
    return held, swapped(held, bits[-1]), order + [r | bits[-1] for r in order]


def halving_order(bits):
    order = [0]
    for bit in reversed(bits):
        order = [r | bit for r in order] + order
    return order


def gathered_back(send, keep, bits):
    for bit in bits[:-1]:
        total = keep + swapped(send, bit).astype(F32)
        half = total.shape[0] // 2
        send, keep = total[:half].astype(BF16), total[half:]
    return keep + swapped(send, bits[-1]).astype(F32)


def route_columns(route, gates):
    high = lax.reduce_precision(gates, 8, 7)
    rest = gates - high
    middle = lax.reduce_precision(rest, 8, 7)
    low = rest - middle
    return [route.astype(BF16), high.astype(BF16), middle.astype(BF16), low.astype(BF16)]


def rows_of(refs, order, wanted, rows, columns=None):
    parts = []
    half = len(order) // 2
    for r in wanted:
        at = order.index(r)
        ref = refs[at // half]
        block = pl.ds(at % half * rows, rows)
        parts.append(ref[block, :] if columns is None else ref[block, columns])
    return jnp.concatenate(parts, axis=0)


def gate_of(words, topk, first, expert):
    words = words.astype(F32)
    at = [words[:, (first + j) * topk : (first + j + 1) * topk] for j in range(4)]
    gates = at[1] + at[2] + at[3]
    chosen = at[0] == expert.astype(F32)
    return jnp.sum(jnp.where(chosen, gates, 0.0), axis=1, keepdims=True)


def times(a, b):
    return lax.dot_general(a, b, (((1,), (0,)), ((), ())), preferred_element_type=F32)


def times_transposed(a, b):
    return lax.dot_general(a, b, (((1,), (1,)), ((), ())), preferred_element_type=F32)


def forward_kernel(
    width, topk, rows, order, back, step, me_ref, xa, xb, gu0, d0, gu1, d1, send_ref, keep_ref
):
    half = len(back) // 2
    for out_ref, wanted in ((send_ref, back[:half]), (keep_ref, back[half:])):
        for start in range(0, half, step):
            now = wanted[start : start + step]
            both = rows_of((xa, xb), order, now, rows)
            x, words = both[:, :width], both[:, width:]
            total = None
            for flip, gu_ref, d_ref in ((0, gu0, d0), (1, gu1, d1)):
                pre = times(x, gu_ref[...])
                hidden_width = pre.shape[1] // 2
                gate, up = pre[:, :hidden_width], pre[:, hidden_width:]
                hidden = (gate * jax.nn.sigmoid(gate) * up).astype(BF16)
                out = times(hidden, d_ref[...]).astype(BF16).astype(F32)
                out = out * gate_of(words, topk, 0, me_ref[0] ^ flip)
                total = out if total is None else total + out
            out_ref[pl.ds(start * rows, len(now) * rows), :] = total.astype(out_ref.dtype)


def backward_kernel(
    topk,
    rows,
    orders,
    back,
    step,
    me_ref,
    wa,
    wb,
    xa,
    xb,
    ca,
    cb,
    gu0,
    d0,
    gu1,
    d1,
    send_ref,
    keep_ref,
):
    half = len(back) // 2
    for out_ref, wanted in ((send_ref, back[:half]), (keep_ref, back[half:])):
        for start in range(0, half, step):
            now = wanted[start : start + step]
            words = rows_of((wa, wb), orders[0], now, rows)
            x = rows_of((xa, xb), orders[1], now, rows)
            cot = rows_of((ca, cb), orders[2], now, rows)
            total = None
            for flip, gu_ref, d_ref in ((0, gu0, d0), (1, gu1, d1)):
                pre = times(x, gu_ref[...])
                hidden_width = pre.shape[1] // 2
                gate, up = pre[:, :hidden_width], pre[:, hidden_width:]
                sig = jax.nn.sigmoid(gate)
                d_hidden = times_transposed(cot, d_ref[...])
                d_gate = d_hidden * up * sig * (1.0 + gate * (1.0 - sig))
                d_up = d_hidden * gate * sig
                both = jnp.concatenate([d_gate.astype(BF16), d_up.astype(BF16)], axis=1)
                out = times_transposed(both, gu_ref[...]).astype(BF16).astype(F32)
                out = out * gate_of(words, topk, 4, me_ref[0] ^ flip)
                total = out if total is None else total + out
            out_ref[pl.ds(start * rows, len(now) * rows), :] = total.astype(out_ref.dtype)


def call(kernel, operands, out_rows, width, flops, words=()):
    whole = pl.BlockSpec(memory_space=pltpu.VMEM)
    specs = [pl.BlockSpec(memory_space=pltpu.SMEM)] + [whole] * (len(operands) - 1)
    for at in words:
        shape = operands[at].shape
        block = (shape[0], shape[1] - width)
        specs[at] = pl.BlockSpec(block, lambda i: (0, width // block[1]))
    shapes = (
        jax.ShapeDtypeStruct((out_rows, width), BF16),
        jax.ShapeDtypeStruct((out_rows, width), F32),
    )
    moved = sum(a.size * a.dtype.itemsize for a in operands)
    return pl.pallas_call(
        kernel,
        grid=(1,),
        out_shape=shapes,
        in_specs=specs,
        out_specs=(whole, whole),
        compiler_params=pltpu.CompilerParams(vmem_limit_bytes=VMEM_LIMIT),
        cost_estimate=pl.CostEstimate(
            flops=flops, bytes_accessed=moved + out_rows * width * 6, transcendentals=0
        ),
    )(*operands)


def on_device(
    x_forward,
    route_forward,
    gate_forward,
    x_backward,
    route_backward,
    gate_backward,
    cotangent,
    w_gate,
    w_up,
    w_down,
):
    experts = lax.axis_size("expert")
    rows, width = x_forward.shape[1:]
    topk = route_forward.shape[2]
    hidden_width = w_gate.shape[3]
    me = lax.axis_index("expert").astype(jnp.int32)

    bits = []
    while 2 << len(bits) < experts:
        bits.insert(0, 2 << len(bits))
    blocks = experts // 2

    columns = route_columns(route_forward[0], gate_forward[0])
    columns += route_columns(route_backward[0], gate_backward[0])
    padding = -(8 * topk) % LANES
    forward_rows = jnp.concatenate(
        [x_forward[0]] + columns + [jnp.zeros((rows, padding), BF16)], axis=1
    )

    gate_up0 = jnp.concatenate([w_gate[0, 0], w_up[0, 0]], axis=1)
    down0 = w_down[0, 0]
    gate_up1, down1 = swapped(gate_up0, 1), swapped(down0, 1)
    weights = (gate_up0, down0, gate_up1, down1)

    fa, fb, forward_order = spread(forward_rows, bits)
    xa, xb, x_order = spread(x_backward[0], bits)
    ca, cb, c_order = spread(cotangent[0], bits)

    back_bits = bits[::-1]
    back = halving_order(back_bits)
    step = min(4, blocks // 2)
    matmul = 2 * blocks * rows * width * hidden_width * 2
    place = jnp.reshape(me, (1,))
    send_f, keep_f = call(
        functools.partial(forward_kernel, width, topk, rows, forward_order, back, step),
        (place, fa, fb) + weights,
        blocks // 2 * rows,
        width,
        3 * matmul,
    )
    layer_out = x_forward[0].astype(F32) + gathered_back(send_f, keep_f, back_bits)
    arrived_forward = passed_along(layer_out.astype(BF16)[None], "section", 1)

    send_b, keep_b = call(
        functools.partial(
            backward_kernel, topk, rows, (forward_order, x_order, c_order), back, step
        ),
        (place, fa, fb, xa, xb, ca, cb) + weights,
        blocks // 2 * rows,
        width,
        5 * matmul,
        words=(1, 2),
    )
    input_grad = cotangent[0].astype(F32) + gathered_back(send_b, keep_b, back_bits)
    arrived_backward = passed_along(input_grad.astype(BF16)[None], "section", -1)
    return (arrived_forward, arrived_backward)


def solution(mesh):
    in_specs = (
        P("section", "expert", None),
        P("section", "expert", None),
        P("section", "expert", None),
        P("section", "expert", None),
        P("section", "expert", None),
        P("section", "expert", None),
        P("section", "expert", None),
        P("section", "expert", None, None),
        P("section", "expert", None, None),
        P("section", "expert", None, None),
    )
    out_specs = (P("section", "expert", None), P("section", "expert", None))
    return jax.shard_map(
        on_device, mesh=mesh, in_specs=in_specs, out_specs=out_specs, check_vma=False
    )
```

```python
import functools

import jax
import jax.numpy as jnp
from jax import lax
from jax.experimental import pallas as pl
from jax.experimental.pallas import tpu as pltpu
from jax.sharding import PartitionSpec as P

F32 = jnp.float32
BF16 = jnp.bfloat16
LANES = 128
VMEM_LIMIT = 48 * 1024 * 1024
COST = 0.1
IN_TURN = "f,Fs,F,Fk,F,b:Fk,c:Fk,Bs,B,Bk,B"
JOIN = False
HBM = True
GU = 1
LITTLE = pl.CostEstimate(flops=1, bytes_accessed=1, transcendentals=0)
PLAN = dict(f="P", b="P", c="P", rf="P", rb="P", odd="QQ", cut="", ops="f,c,b,f,c,b,f,c,b,Fs,F,Fk,Bs,B,F,Bk:F0,B,F,B", step=4)


def passed_along(block, distance, paths, bit=0):
    sections, experts = lax.axis_size("section"), lax.axis_size("expert")
    route = [
        (s * experts + e, (s + distance) % sections * experts + (e ^ paths[e % 2].get(bit, 0)))
        for s in range(sections)
        for e in range(experts)
    ]
    return lax.ppermute(block, ("section", "expert"), route)


def swapped(block, paths, bit):
    route = [(i, i ^ paths[i % 2][bit]) for i in range(lax.axis_size("expert"))]
    return lax.ppermute(block, "expert", route)


class Spread:
    def __init__(self, block, paths, bits, cut):
        self.paths, self.bits, self.cut, self.came, self.held, self.order = paths, bits, cut, [], block, [0]
        self.parts, self.orders = [], []

    def done(self):
        return len(self.came) == len(self.bits) + self.cut

    def step(self, after=()):
        at, last = len(self.came), len(self.bits) - 1
        bit = self.bits[min(at, last)]
        if at <= last:
            parts = [self.held] + ([self.came[-1]] if 0 < at and (at < last or not self.cut) else [])
            parts = behind(parts, after)
            if len(parts) > 1:
                self.held = joined(parts, 0) if JOIN else jnp.concatenate(parts, axis=0)
                self.order = self.order + [r | self.bits[at - 1] for r in self.order]
            else:
                self.held = parts[0]
            payload, order = self.held, self.order
        else:
            (payload,) = behind([self.came[last - 1]], after)
            order = [r | self.bits[last - 1] for r in self.order]
        self.came.append(swapped(payload, self.paths, bit))
        if at >= last:
            self.parts += [payload, self.came[-1]]
            self.orders += [order, [r | bit for r in order]]


def behind(arrays, others):
    if not others:
        return list(arrays)
    return list(lax.optimization_barrier((*arrays, *others))[: len(arrays)])


def joining_kernel(axis, *refs):
    *parts, out_ref, sems = refs
    at, copies = 0, []
    for number, part in enumerate(parts):
        here = [slice(None)] * 2
        here[axis] = pl.ds(at, part.shape[axis])
        copies.append(pltpu.make_async_copy(part, out_ref.at[tuple(here)], sems.at[number]))
        copies[-1].start()
        at += part.shape[axis]
    for copy in copies:
        copy.wait()


def joined(parts, axis):
    shape = list(parts[0].shape)
    shape[axis] = sum(part.shape[axis] for part in parts)
    return pl.pallas_call(
        functools.partial(joining_kernel, axis),
        out_shape=jax.ShapeDtypeStruct(tuple(shape), parts[0].dtype),
        in_specs=[pl.BlockSpec(memory_space=pl.ANY)] * len(parts),
        out_specs=pl.BlockSpec(memory_space=pltpu.VMEM),
        scratch_shapes=[pltpu.SemaphoreType.DMA((len(parts),))],
        cost_estimate=LITTLE,
    )(*parts)


def halving_order(bits):
    order = [0]
    for bit in reversed(bits):
        order = [r | bit for r in order] + order
    return order


class Return:
    def __init__(self, sends, paths, bits, distance):
        self.sends, self.keep, self.came = sends, None, []
        self.paths, self.bits, self.distance = paths, bits, distance

    def done(self):
        return len(self.came) == len(self.bits) + len(self.sends)

    def step(self, after=()):
        at, first = len(self.came), len(self.sends)
        if at < first:
            (send,) = behind([self.sends[at]], after)
            self.came.append(swapped(send, self.paths, self.bits[0]))
            return
        if at == first and first == 2:
            half = self.keep.shape[0] // 2
            send, self.keep = self.keep[:half] + self.came[0].astype(F32), self.keep[half:]
        else:
            total = self.keep + self.came[-1].astype(F32)
            if at == 3 and first == 2:
                total = total + self.came[1].astype(F32)
            half = total.shape[0] // 2
            send, self.keep = total[:half], total[half:]
        bit = self.bits[at - first + 1]
        if bit != self.bits[-1]:
            (send,) = behind([send.astype(BF16)], after)
            self.came.append(swapped(send, self.paths, bit))
        else:
            send, keep = behind([send.astype(BF16), self.keep.astype(BF16)], after)
            self.came.append(passed_along(keep, self.distance, self.paths))
            self.came.append(passed_along(send, self.distance, self.paths, bit))


def packing_kernel(x_ref, route_f, gate_f, route_b, gate_b, out_ref):
    width, extra = x_ref.shape[1], out_ref.shape[1] - x_ref.shape[1]
    out_ref[:, :width] = x_ref[...]
    pieces = []
    for route_ref, gate_ref in ((route_f, gate_f), (route_b, gate_b)):
        pieces.append(route_ref[...].astype(F32))
        rest = gate_ref[...]
        for _ in range(3):
            pieces.append(rest.astype(BF16).astype(F32))
            rest = rest - pieces[-1]
    used = sum(piece.shape[0] for piece in pieces)
    if extra > used:
        pieces.append(jnp.zeros((extra - used, x_ref.shape[0]), F32))
    out_ref[:, width:] = jnp.transpose(jnp.concatenate(pieces, axis=0)).astype(BF16)


def packed(rows, *words):
    length, width = rows.shape
    extra = 8 * words[0].shape[1]
    return pl.pallas_call(
        packing_kernel,
        out_shape=jax.ShapeDtypeStruct((length, width + extra + -extra % LANES), BF16),
        cost_estimate=LITTLE,
    )(rows, *[jnp.transpose(array) for array in words])


def gate_of(words, topk, first, expert):
    words = words.astype(F32)
    at = [words[:, (first + j) * topk : (first + j + 1) * topk] for j in range(4)]
    gates = at[1] + at[2] + at[3]
    chosen = at[0] == expert.astype(F32)
    return jnp.sum(jnp.where(chosen, gates, 0.0), axis=1, keepdims=True)


def times(a, b):
    return lax.dot_general(a, b, (((1,), (0,)), ((), ())), preferred_element_type=F32)


def times_transposed(a, b):
    return lax.dot_general(a, b, (((1,), (1,)), ((), ())), preferred_element_type=F32)


def forward_rows(x, gate_up, down):
    pre = times(x, gate_up[...])
    width = pre.shape[1] // 2
    gate, up = pre[:, :width], pre[:, width:]
    hidden = (gate * jax.nn.sigmoid(gate) * up).astype(BF16)
    return times(hidden, down[...])


def backward_rows(x, cot, gate_up, down):
    pre = times(x, gate_up[...])
    width = pre.shape[1] // 2
    gate, up = pre[:, :width], pre[:, width:]
    sig = jax.nn.sigmoid(gate)
    d_hidden = times_transposed(cot, down[...])
    d_gate = d_hidden * up * sig * (1.0 + gate * (1.0 - sig))
    d_up = d_hidden * gate * sig
    both = jnp.concatenate([d_gate.astype(BF16), d_up.astype(BF16)], axis=1)
    return times_transposed(both, gate_up[...])


def expert_kernel(each, topk, first, rows, step, copies, me_ref, *refs):
    count = 1 + max(operand for each_copy in copies for operand, *_ in each_copy)
    buffers, sems = refs[-1 - len(copies) : -1], refs[-1]
    out_refs = refs[count : -1 - len(copies)]
    started = []
    for buffer, pieces in zip(buffers, copies, strict=True):
        row, group = 0, []
        for operand, at, length, column in pieces:
            copy = pltpu.make_async_copy(
                refs[operand].at[pl.ds(at, length), pl.ds(column, buffer.shape[1])],
                buffer.at[pl.ds(row, length), :],
                sems.at[sum(map(len, started)) + len(group)],
            )
            copy.start()
            group.append(copy)
            row += length
        started.append(group)

    def ready(number):
        for copy in started[number]:
            copy.wait()
        started[number] = []
        return buffers[number]

    inputs = len(copies) - 5
    length = out_refs[0].shape[0]
    total_rows = buffers[0].shape[0]
    totals = {}
    for flip in range(2):
        for start in range(0, total_rows, step * rows):
            tile = pl.ds(start, min(step * rows, total_rows - start))
            taken = [ready(number)[tile, :] for number in range(inputs)]
            gate_up, down = ready(inputs + 2 * flip), ready(inputs + 2 * flip + 1)
            out = each(*taken, gate_up, down).astype(BF16).astype(F32)
            out = out * gate_of(ready(len(copies) - 1)[tile, :], topk, first, me_ref[0] ^ flip)
            if flip == 0:
                totals[start] = out
                continue
            out = (totals[start] + out).astype(out_refs[0].dtype)
            for at in range(0, out.shape[0], rows):
                number, row = divmod(start + at, length)
                out_refs[number][pl.ds(row, rows), :] = out[at : at + rows]


def weighted(each, first, topk, rows, step, wanted, dtype, outputs, place, words, inputs, weights):
    width, hidden_width = weights[1].shape[1], weights[1].shape[0]
    operands, copies, scratch = [], [], []
    length = len(wanted) * rows

    def operand(array):
        for number, other in enumerate(operands):
            if other is array:
                return number
        operands.append(array)
        return len(operands) - 1

    def rows_from(parts, orders, columns, column):
        pieces = []
        for r in wanted:
            part, block = next((n, o.index(r)) for n, o in enumerate(orders) if r in o)
            number, at = operand(parts[part]), block * rows
            if pieces and pieces[-1][0] == number and pieces[-1][1] + pieces[-1][2] == at:
                pieces[-1] = (number, pieces[-1][1], pieces[-1][2] + rows, column)
            else:
                pieces.append((number, at, rows, column))
        copies.append(pieces)
        scratch.append(pltpu.VMEM((length, columns), BF16))

    for parts, orders in inputs:
        rows_from(parts, orders, width, 0)
    for array in weights:
        copies.append([(operand(array), 0, array.shape[0], 0)])
        scratch.append(pltpu.VMEM(array.shape, BF16))
    rows_from(*words, width)
    return pl.pallas_call(
        functools.partial(expert_kernel, each, topk, first, rows, step, copies),
        out_shape=[jax.ShapeDtypeStruct((length // outputs, width), dtype)] * outputs,
        in_specs=[pl.BlockSpec(memory_space=pltpu.SMEM)]
        + [pl.BlockSpec(memory_space=pltpu.HBM if HBM else pl.ANY)] * len(operands),
        out_specs=[pl.BlockSpec(memory_space=pltpu.VMEM)] * outputs,
        scratch_shapes=scratch + [pltpu.SemaphoreType.DMA((sum(map(len, copies)),))],
        compiler_params=pltpu.CompilerParams(vmem_limit_bytes=VMEM_LIMIT),
        cost_estimate=pl.CostEstimate(
            flops=int(COST * 4 * (2 * len(inputs) + 1) * length * width * hidden_width),
            bytes_accessed=int(COST * sum(a.size * a.dtype.itemsize for a in operands)),
            transcendentals=0,
        ),
    )(place, *operands)


def on_device(
    x_forward,
    route_forward,
    gate_forward,
    x_backward,
    route_backward,
    gate_backward,
    cotangent,
    w_gate,
    w_up,
    w_down,
):
    experts = lax.axis_size("expert")
    rows, width = x_forward.shape[1:]
    topk = route_forward.shape[2]
    me = lax.axis_index("expert").astype(jnp.int32)

    bits = []
    while 2 << len(bits) < experts:
        bits.insert(0, 2 << len(bits))
    blocks = experts // 2
    orders = {
        "P": bits,
        "Q": bits[:-2] + [bits[-1], bits[-2]],
        "R": bits[-1:] + bits[:-1],
    }
    plan = PLAN
    even = dict(zip(bits, bits))
    odd = {kind: dict(zip(bits, orders[plan["odd"][kind != "f"]])) for kind in "fbc"}
    paths = {kind: (even, odd[kind]) for kind in "fbc"}

    arrays = {"f": x_forward[0], "b": x_backward[0], "c": cotangent[0]}
    words = [route_forward[0], gate_forward[0], route_backward[0], gate_backward[0]]
    held = {}

    arrays["f"] = packed(arrays["f"], *words)
    down0 = w_down[0, 0]
    pair = [w_gate[0, 0], w_up[0, 0]]
    if GU:
        *pair, down0 = behind([*pair, down0], [arrays["f"]])
    gate_up0 = jnp.concatenate(pair, axis=1)
    chip = [{1: 1}] * 2
    gate_up1, down1 = swapped(gate_up0, chip, 1), swapped(down0, chip, 1)
    weights = [gate_up0, down0, gate_up1, down1]

    step = min(plan["step"], blocks // 2)
    place = jnp.reshape(me, (1,))

    class Far:
        came = [passed_along(x_forward[0], 1, [{}, {}]), passed_along(cotangent[0], -1, [{}, {}])]

    held["y"] = Far

    def arrived(far, kind):
        one, other = held[kind].came[-2:]
        return (far.astype(F32) + (one.astype(F32) + other.astype(F32))).astype(BF16)[None]

    outs = {}
    items = (plan["ops"] if len(bits) < 4 else IN_TURN).split(",")
    left = {name: [item[0] for item in items if item[1:2] not in ("s", "k")].count(name) for name in "fbcFB"}
    for item in items:
        name, _, after = item.partition(":")
        after = [
            outs[other] if other in outs else held[other[0]].came[int(other[1])]
            for other in after.split()
        ]
        kind = name[0].lower()
        if len(name) == 1:
            if name not in held:
                held[name] = Spread(arrays[name], paths[kind], orders[plan[name]], name in plan["cut"])
            held[name].step(after)
            left[name] -= 1
            while left[name] == 0 and not held[name].done():
                held[name].step()
            continue
        back = orders[plan["r" + kind]][::-1]
        order = halving_order(back)
        takes = [(held[other].parts, held[other].orders) for other in ("f" if kind == "f" else "bc")]
        carrier = (held["f"].parts, held["f"].orders, held["f"].held.shape[1] - width)
        each, first = (forward_rows, 0) if kind == "f" else (backward_rows, 4)
        half = len(order) // 2
        sent = name[1] == "s"
        wanted, dtype = (order[:half], BF16) if sent else (order[half:], F32)
        (place,) = behind([place], after)
        number = 2 if sent and name[0] in plan["cut"] else 1
        out = weighted(
            each, first, topk, rows, step, wanted, dtype, number, place, carrier, takes, weights
        )
        place, *out = lax.optimization_barrier((place, *out))
        outs[name] = out[0]
        if sent:
            held[name[0]] = Return(out, paths[kind], back, 1 if kind == "f" else -1)
        else:
            held[name[0]].keep = out[0]

    return arrived(held["y"].came[0], "F"), arrived(held["y"].came[1], "B")


def solution(mesh):
    in_specs = (
        P("section", "expert", None),
        P("section", "expert", None),
        P("section", "expert", None),
        P("section", "expert", None),
        P("section", "expert", None),
        P("section", "expert", None),
        P("section", "expert", None),
        P("section", "expert", None, None),
        P("section", "expert", None, None),
        P("section", "expert", None, None),
    )
    out_specs = (P("section", "expert", None), P("section", "expert", None))
    return jax.shard_map(
        on_device, mesh=mesh, in_specs=in_specs, out_specs=out_specs, check_vma=False
    )
```

```python
import functools

import jax
import jax.numpy as jnp
from jax import lax
from jax.experimental import pallas as pl
from jax.experimental.pallas import tpu as pltpu
from jax.sharding import PartitionSpec as P

F32 = jnp.float32
BF16 = jnp.bfloat16
LANES = 128
VMEM_LIMIT = 20 * 1024 * 1024
COST = 1.0
IN_TURN = "f,Fs,F,Fk,F,b:Fk,c:Fk,Bs,B,Bk,B"
JOIN = False
LOAD = True
HBM = False
GU = 1
LITTLE = pl.CostEstimate(flops=1, bytes_accessed=1, transcendentals=0)
PLAN = dict(f="P", b="P", c="P", rf="P", rb="P", odd="QQ", cut="FB", ops="f,c,b,f,c,b,f,c:W,b,Fs,F,F,Fk,Bs,B,B,F,Bk:F0,B,F,B", step=4)


def passed_along(block, distance, paths, bit=0):
    sections, experts = lax.axis_size("section"), lax.axis_size("expert")
    route = [
        (s * experts + e, (s + distance) % sections * experts + (e ^ paths[e % 2].get(bit, 0)))
        for s in range(sections)
        for e in range(experts)
    ]
    return lax.ppermute(block, ("section", "expert"), route)


def swapped(block, paths, bit):
    route = [(i, i ^ paths[i % 2][bit]) for i in range(lax.axis_size("expert"))]
    return lax.ppermute(block, "expert", route)


class Spread:
    def __init__(self, block, paths, bits, cut):
        self.paths, self.bits, self.cut, self.came, self.held, self.order = paths, bits, cut, [], block, [0]
        self.parts, self.orders = [], []

    def done(self):
        return len(self.came) == len(self.bits) + self.cut

    def step(self, after=()):
        at, last = len(self.came), len(self.bits) - 1
        bit = self.bits[min(at, last)]
        if at <= last:
            parts = [self.held] + ([self.came[-1]] if 0 < at and (at < last or not self.cut) else [])
            parts = behind(parts, after)
            if len(parts) > 1:
                self.held = joined(parts, 0) if JOIN else jnp.concatenate(parts, axis=0)
                self.order = self.order + [r | self.bits[at - 1] for r in self.order]
            else:
                self.held = parts[0]
            payload, order = self.held, self.order
        else:
            (payload,) = behind([self.came[last - 1]], after)
            order = [r | self.bits[last - 1] for r in self.order]
        self.came.append(swapped(payload, self.paths, bit))
        if at >= last:
            self.parts += [payload, self.came[-1]]
            self.orders += [order, [r | bit for r in order]]


def behind(arrays, others):
    if not others:
        return list(arrays)
    return list(lax.optimization_barrier((*arrays, *others))[: len(arrays)])


def joining_kernel(axis, *refs):
    *parts, out_ref, sems = refs
    at, copies = 0, []
    for number, part in enumerate(parts):
        here = [slice(None)] * 2
        here[axis] = pl.ds(at, part.shape[axis])
        copies.append(pltpu.make_async_copy(part, out_ref.at[tuple(here)], sems.at[number]))
        copies[-1].start()
        at += part.shape[axis]
    for copy in copies:
        copy.wait()


def joined(parts, axis):
    shape = list(parts[0].shape)
    shape[axis] = sum(part.shape[axis] for part in parts)
    return pl.pallas_call(
        functools.partial(joining_kernel, axis),
        out_shape=jax.ShapeDtypeStruct(tuple(shape), parts[0].dtype),
        in_specs=[pl.BlockSpec(memory_space=pl.ANY)] * len(parts),
        out_specs=pl.BlockSpec(memory_space=pltpu.VMEM),
        scratch_shapes=[pltpu.SemaphoreType.DMA((len(parts),))],
        cost_estimate=LITTLE,
    )(*parts)


def halving_order(bits):
    order = [0]
    for bit in reversed(bits):
        order = [r | bit for r in order] + order
    return order


class Return:
    def __init__(self, sends, paths, bits, distance):
        self.sends, self.keep, self.came = sends, None, []
        self.paths, self.bits, self.distance = paths, bits, distance

    def done(self):
        return len(self.came) == len(self.bits) + len(self.sends)

    def step(self, after=()):
        at, first = len(self.came), len(self.sends)
        if at < first:
            (send,) = behind([self.sends[at]], after)
            self.came.append(swapped(send, self.paths, self.bits[0]))
            return
        if at == first and first == 2:
            half = self.keep.shape[0] // 2
            send, self.keep = self.keep[:half] + self.came[0].astype(F32), self.keep[half:]
        else:
            total = self.keep + self.came[-1].astype(F32)
            if at == 3 and first == 2:
                total = total + self.came[1].astype(F32)
            half = total.shape[0] // 2
            send, self.keep = total[:half], total[half:]
        bit = self.bits[at - first + 1]
        if bit != self.bits[-1]:
            (send,) = behind([send.astype(BF16)], after)
            self.came.append(swapped(send, self.paths, bit))
        else:
            send, keep = behind([send.astype(BF16), self.keep.astype(BF16)], after)
            self.came.append(passed_along(keep, self.distance, self.paths))
            self.came.append(passed_along(send, self.distance, self.paths, bit))


def packing_kernel(x_ref, route_f, gate_f, route_b, gate_b, out_ref):
    width, extra = x_ref.shape[1], out_ref.shape[1] - x_ref.shape[1]
    out_ref[:, :width] = x_ref[...]
    pieces = []
    for route_ref, gate_ref in ((route_f, gate_f), (route_b, gate_b)):
        pieces.append(route_ref[...].astype(F32))
        rest = gate_ref[...]
        for _ in range(3):
            pieces.append(rest.astype(BF16).astype(F32))
            rest = rest - pieces[-1]
    used = sum(piece.shape[0] for piece in pieces)
    if extra > used:
        pieces.append(jnp.zeros((extra - used, x_ref.shape[0]), F32))
    out_ref[:, width:] = jnp.transpose(jnp.concatenate(pieces, axis=0)).astype(BF16)


def packed(rows, *words):
    length, width = rows.shape
    extra = 8 * words[0].shape[1]
    return pl.pallas_call(
        packing_kernel,
        out_shape=jax.ShapeDtypeStruct((length, width + extra + -extra % LANES), BF16),
        cost_estimate=LITTLE,
    )(rows, *[jnp.transpose(array) for array in words])


def gate_of(words, topk, first, expert):
    words = words.astype(F32)
    at = [words[:, (first + j) * topk : (first + j + 1) * topk] for j in range(4)]
    gates = at[1] + at[2] + at[3]
    chosen = at[0] == expert.astype(F32)
    return jnp.sum(jnp.where(chosen, gates, 0.0), axis=1, keepdims=True)


def times(a, b):
    return lax.dot_general(a, b, (((1,), (0,)), ((), ())), preferred_element_type=F32)


def times_transposed(a, b):
    return lax.dot_general(a, b, (((1,), (1,)), ((), ())), preferred_element_type=F32)


def forward_rows(x, gate_up, down):
    pre = times(x, gate_up[...])
    width = pre.shape[1] // 2
    gate, up = pre[:, :width], pre[:, width:]
    hidden = (gate * jax.nn.sigmoid(gate) * up).astype(BF16)
    return times(hidden, down[...])


def backward_rows(x, cot, gate_up, down):
    pre = times(x, gate_up[...])
    width = pre.shape[1] // 2
    gate, up = pre[:, :width], pre[:, width:]
    sig = jax.nn.sigmoid(gate)
    d_hidden = times_transposed(cot, down[...])
    d_gate = d_hidden * up * sig * (1.0 + gate * (1.0 - sig))
    d_up = d_hidden * gate * sig
    both = jnp.concatenate([d_gate.astype(BF16), d_up.astype(BF16)], axis=1)
    return times_transposed(both, gate_up[...])


def loading_kernel(*refs):
    sems = refs[-1]
    count = len(refs) // 2
    copies = [pltpu.make_async_copy(refs[n], refs[count + n], sems.at[n]) for n in range(count)]
    for copy in copies:
        copy.start()
    for copy in copies:
        copy.wait()


def loaded(arrays):
    return pl.pallas_call(
        loading_kernel,
        out_shape=[jax.ShapeDtypeStruct(array.shape, array.dtype) for array in arrays],
        in_specs=[pl.BlockSpec(memory_space=pl.ANY)] * len(arrays),
        out_specs=[pl.BlockSpec(memory_space=pltpu.VMEM)] * len(arrays),
        scratch_shapes=[pltpu.SemaphoreType.DMA((len(arrays),))],
        compiler_params=pltpu.CompilerParams(vmem_limit_bytes=VMEM_LIMIT),
        cost_estimate=LITTLE,
    )(*arrays)


def expert_kernel(each, topk, first, rows, step, copies, me_ref, *refs):
    count = 1 + max(operand for each_copy in copies for operand, *_ in each_copy)
    buffers, sems = refs[-1 - len(copies) : -1], refs[-1]
    weights, out_refs = refs[count : count + 4], refs[count + 4 : -1 - len(copies)]
    begins = [0]
    for pieces in copies:
        begins.append(begins[-1] + len(pieces))
    started = {}

    def start_copies(number):
        buffer, row = buffers[number], 0
        started[number] = []
        for piece, (operand, at, length, column) in enumerate(copies[number]):
            copy = pltpu.make_async_copy(
                refs[operand].at[pl.ds(at, length), pl.ds(column, buffer.shape[1])],
                buffer.at[pl.ds(row, length), :],
                sems.at[begins[number] + piece],
            )
            copy.start()
            started[number].append(copy)
            row += length

    def ready(number):
        for copy in started[number]:
            copy.wait()
        started[number] = []
        return buffers[number]

    inputs = len(copies) - 1
    for number in range(len(copies)):
        start_copies(number)
    total_rows = buffers[0].shape[0]
    places = [(out_ref, row) for out_ref in out_refs for row in range(0, out_ref.shape[0], rows)]
    totals = {}
    for flip in range(2):
        for start in range(0, total_rows, step * rows):
            tile = pl.ds(start, min(step * rows, total_rows - start))
            taken = [ready(number)[tile, :] for number in range(inputs)]
            gate_up, down = weights[2 * flip : 2 * flip + 2]
            out = each(*taken, gate_up, down).astype(BF16).astype(F32)
            out = out * gate_of(ready(len(copies) - 1)[tile, :], topk, first, me_ref[0] ^ flip)
            if flip == 0:
                totals[start] = out
                continue
            out = totals[start] + out
            for at in range(0, out.shape[0], rows):
                out_ref, row = places[(start + at) // rows]
                out_ref[pl.ds(row, rows), :] = out[at : at + rows].astype(out_ref.dtype)


def weighted(each, first, topk, rows, step, wanted, outputs, place, words, inputs, weights):
    width, hidden_width = weights[1].shape[1], weights[1].shape[0]
    operands, copies, scratch = [], [], []
    length = len(wanted) * rows

    def operand(array):
        for number, other in enumerate(operands):
            if other is array:
                return number
        operands.append(array)
        return len(operands) - 1

    def rows_from(parts, orders, columns, column):
        pieces = []
        for r in wanted:
            part, block = next((n, o.index(r)) for n, o in enumerate(orders) if r in o)
            number, at = operand(parts[part]), block * rows
            if pieces and pieces[-1][0] == number and pieces[-1][1] + pieces[-1][2] == at:
                pieces[-1] = (number, pieces[-1][1], pieces[-1][2] + rows, column)
            else:
                pieces.append((number, at, rows, column))
        copies.append(pieces)
        scratch.append(pltpu.VMEM((length, columns), BF16))

    for parts, orders in inputs:
        rows_from(parts, orders, width, 0)
    rows_from(*words, width)
    return pl.pallas_call(
        functools.partial(expert_kernel, each, topk, first, rows, step, copies),
        out_shape=[jax.ShapeDtypeStruct((number * rows, width), dtype) for number, dtype in outputs],
        in_specs=[pl.BlockSpec(memory_space=pltpu.SMEM)]
        + [pl.BlockSpec(memory_space=pltpu.HBM if HBM else pl.ANY)] * len(operands)
        + [pl.BlockSpec(memory_space=pltpu.VMEM)] * len(weights),
        out_specs=[pl.BlockSpec(memory_space=pltpu.VMEM)] * len(outputs),
        scratch_shapes=scratch + [pltpu.SemaphoreType.DMA((sum(map(len, copies)),))],
        compiler_params=pltpu.CompilerParams(vmem_limit_bytes=VMEM_LIMIT),
        cost_estimate=pl.CostEstimate(
            flops=int(COST * 4 * (2 * len(inputs) + 1) * length * width * hidden_width),
            bytes_accessed=int(COST * sum(a.size * a.dtype.itemsize for a in operands)),
            transcendentals=0,
        ),
    )(place, *operands, *weights)


def on_device(
    x_forward,
    route_forward,
    gate_forward,
    x_backward,
    route_backward,
    gate_backward,
    cotangent,
    w_gate,
    w_up,
    w_down,
):
    experts = lax.axis_size("expert")
    rows, width = x_forward.shape[1:]
    topk = route_forward.shape[2]
    me = lax.axis_index("expert").astype(jnp.int32)

    bits = []
    while 2 << len(bits) < experts:
        bits.insert(0, 2 << len(bits))
    blocks = experts // 2
    orders = {
        "P": bits,
        "Q": bits[:-2] + [bits[-1], bits[-2]],
        "R": bits[-1:] + bits[:-1],
    }
    plan = PLAN
    even = dict(zip(bits, bits))
    odd = {kind: dict(zip(bits, orders[plan["odd"][kind != "f"]])) for kind in "fbc"}
    paths = {kind: (even, odd[kind]) for kind in "fbc"}

    arrays = {"f": x_forward[0], "b": x_backward[0], "c": cotangent[0]}
    words = [route_forward[0], gate_forward[0], route_backward[0], gate_backward[0]]
    held = {}

    arrays["f"] = packed(arrays["f"], *words)
    down0 = w_down[0, 0]
    pair = [w_gate[0, 0], w_up[0, 0]]
    if GU == 1:
        *pair, down0 = behind([*pair, down0], [arrays["f"]])
    if GU in ("f", "b", "c"):
        held[GU] = Spread(arrays[GU], paths[GU], orders[plan[GU]], GU in plan["cut"])
        held[GU].step()
        *pair, down0 = behind([*pair, down0], held[GU].came)
    gate_up0 = jnp.concatenate(pair, axis=1)
    chip = [{1: 1}] * 2
    gate_up1, down1 = swapped(gate_up0, chip, 1), swapped(down0, chip, 1)
    weights = [gate_up0, down0, gate_up1, down1]
    if LOAD:
        weights = loaded(weights)

    step = min(plan["step"], blocks // 2)
    place = jnp.reshape(me, (1,))

    class Far:
        came = [passed_along(x_forward[0], 1, [{}, {}]), passed_along(cotangent[0], -1, [{}, {}])]

    held["y"] = Far

    def arrived(far, kind):
        one, other = held[kind].came[-2:]
        return (far.astype(F32) + (one.astype(F32) + other.astype(F32))).astype(BF16)[None]

    outs, keeps = {"W": weights[0]}, {}
    items = (plan["ops"] if len(bits) < 4 else IN_TURN).split(",")
    left = {name: [item[0] for item in items if item[1:2] not in ("s", "k", "a")].count(name) for name in "fbcFB"}
    first_left = dict(left)
    for item in items:
        name, _, after = item.partition(":")
        after = [
            outs[other] if other in outs else held[other[0]].came[int(other[1])]
            for other in after.split()
        ]
        kind = name[0].lower()
        if len(name) == 1:
            if name not in held:
                held[name] = Spread(arrays[name], paths[kind], orders[plan[name]], name in plan["cut"])
            if name != GU or left[name] < first_left[name]:
                held[name].step(after)
            left[name] -= 1
            while left[name] == 0 and not held[name].done():
                held[name].step()
            continue
        back = orders[plan["r" + kind]][::-1]
        order = halving_order(back)
        takes = [(held[other].parts, held[other].orders) for other in ("f" if kind == "f" else "bc")]
        carrier = (held["f"].parts, held["f"].orders, held["f"].held.shape[1] - width)
        each, first = (forward_rows, 0) if kind == "f" else (backward_rows, 4)
        half = len(order) // 2
        sends = [(half // 2, BF16)] * 2 if name[0] in plan["cut"] else [(half, BF16)]
        wanted, results = {
            "s": (order[:half], sends),
            "k": (order[half:], [(half, F32)]),
            "a": (order, sends + [(half, F32)]),
        }[name[1]]
        (place,) = behind([place], after)
        out = weighted(each, first, topk, rows, step, wanted, results, place, carrier, takes, weights)
        place, *out = lax.optimization_barrier((place, *out))
        outs[name] = out[0]
        keeps[name[0]] = keeps.get(name[0]) if name[1] == "s" else out.pop()
        if name[1] != "k":
            held[name[0]] = Return(out, paths[kind], back, 1 if kind == "f" else -1)
        if name[0] in held:
            held[name[0]].keep = keeps[name[0]]

    return arrived(held["y"].came[0], "F"), arrived(held["y"].came[1], "B")


def solution(mesh):
    in_specs = (
        P("section", "expert", None),
        P("section", "expert", None),
        P("section", "expert", None),
        P("section", "expert", None),
        P("section", "expert", None),
        P("section", "expert", None),
        P("section", "expert", None),
        P("section", "expert", None, None),
        P("section", "expert", None, None),
        P("section", "expert", None, None),
    )
    out_specs = (P("section", "expert", None), P("section", "expert", None))
    return jax.shard_map(
        on_device, mesh=mesh, in_specs=in_specs, out_specs=out_specs, check_vma=False
    )
```

```python
import functools

import jax
import jax.numpy as jnp
from jax import lax
from jax.experimental import pallas as pl
from jax.experimental.pallas import tpu as pltpu
from jax.sharding import PartitionSpec as P

F32 = jnp.float32
BF16 = jnp.bfloat16
LANES = 128
VMEM_LIMIT = 20 * 1024 * 1024
TOGETHER = "f,c,b,f,c,b,f,c,b,Fs,F,F,Fk,Bs,B,B,F,Bk,B,F,B"
IN_TURN = "f,Fs,F,Fk,F,b:Fk,c:Fk,Bs,B,Bk,B"
LITTLE = pl.CostEstimate(flops=1, bytes_accessed=1, transcendentals=0)


def passed_along(block, distance, paths, bit=0):
    sections, experts = lax.axis_size("section"), lax.axis_size("expert")
    route = [
        (s * experts + e, (s + distance) % sections * experts + (e ^ paths[e % 2].get(bit, 0)))
        for s in range(sections)
        for e in range(experts)
    ]
    return lax.ppermute(block, ("section", "expert"), route)


def swapped(block, paths, bit):
    route = [(i, i ^ paths[i % 2][bit]) for i in range(lax.axis_size("expert"))]
    return lax.ppermute(block, "expert", route)


class Spread:
    def __init__(self, block, paths, bits):
        self.paths, self.bits = paths, bits
        self.came, self.held, self.order = [], block, [0]

    def done(self):
        return len(self.came) == len(self.bits)

    def step(self, after=()):
        at = len(self.came)
        parts = behind([self.held] + self.came[-1:], after)
        self.held = parts[0] if at == 0 else jnp.concatenate(parts, axis=0)
        if at:
            self.order = self.order + [r | self.bits[at - 1] for r in self.order]
        self.came.append(swapped(self.held, self.paths, self.bits[at]))
        self.parts = [self.held, self.came[-1]]
        self.orders = [self.order, [r | self.bits[at] for r in self.order]]


def behind(arrays, others):
    if not others:
        return list(arrays)
    return list(lax.optimization_barrier((*arrays, *others))[: len(arrays)])


def halving_order(bits):
    order = [0]
    for bit in reversed(bits):
        order = [r | bit for r in order] + order
    return order


class Return:
    def __init__(self, sends, paths, bits, distance):
        self.sends, self.keep, self.came = sends, None, []
        self.paths, self.bits, self.distance = paths, bits, distance

    def done(self):
        return len(self.came) == len(self.bits) + 2

    def step(self, after=()):
        at = len(self.came)
        if at < 2:
            (send,) = behind([self.sends[at]], after)
            self.came.append(swapped(send, self.paths, self.bits[0]))
            return
        half = self.keep.shape[0] // 2
        if at == 2:
            send, self.keep = self.keep[:half] + self.came[0].astype(F32), self.keep[half:]
        else:
            total = self.keep + self.came[-1].astype(F32)
            if at == 3:
                total = total + self.came[1].astype(F32)
            half = total.shape[0] // 2
            send, self.keep = total[:half], total[half:]
        bit = self.bits[at - 1]
        if bit != self.bits[-1]:
            (send,) = behind([send.astype(BF16)], after)
            self.came.append(swapped(send, self.paths, bit))
        else:
            send, keep = behind([send.astype(BF16), self.keep.astype(BF16)], after)
            self.came.append(passed_along(keep, self.distance, self.paths))
            self.came.append(passed_along(send, self.distance, self.paths, bit))


def packing_kernel(x_ref, route_f, gate_f, route_b, gate_b, out_ref):
    width, extra = x_ref.shape[1], out_ref.shape[1] - x_ref.shape[1]
    out_ref[:, :width] = x_ref[...]
    pieces = []
    for route_ref, gate_ref in ((route_f, gate_f), (route_b, gate_b)):
        pieces.append(route_ref[...].astype(F32))
        rest = gate_ref[...]
        for _ in range(3):
            pieces.append(rest.astype(BF16).astype(F32))
            rest = rest - pieces[-1]
    used = sum(piece.shape[0] for piece in pieces)
    if extra > used:
        pieces.append(jnp.zeros((extra - used, x_ref.shape[0]), F32))
    out_ref[:, width:] = jnp.transpose(jnp.concatenate(pieces, axis=0)).astype(BF16)


def packed(rows, *words):
    length, width = rows.shape
    extra = 8 * words[0].shape[1]
    return pl.pallas_call(
        packing_kernel,
        out_shape=jax.ShapeDtypeStruct((length, width + extra + -extra % LANES), BF16),
        cost_estimate=LITTLE,
    )(rows, *[jnp.transpose(array) for array in words])


def gate_of(words, topk, first, expert):
    words = words.astype(F32)
    at = [words[:, (first + j) * topk : (first + j + 1) * topk] for j in range(4)]
    gates = at[1] + at[2] + at[3]
    chosen = at[0] == expert.astype(F32)
    return jnp.sum(jnp.where(chosen, gates, 0.0), axis=1, keepdims=True)


def times(a, b):
    return lax.dot_general(a, b, (((1,), (0,)), ((), ())), preferred_element_type=F32)


def times_transposed(a, b):
    return lax.dot_general(a, b, (((1,), (1,)), ((), ())), preferred_element_type=F32)


def forward_rows(x, gate_up, down):
    pre = times(x, gate_up[...])
    width = pre.shape[1] // 2
    gate, up = pre[:, :width], pre[:, width:]
    hidden = (gate * jax.nn.sigmoid(gate) * up).astype(BF16)
    return times(hidden, down[...])


def backward_rows(x, cot, gate_up, down):
    pre = times(x, gate_up[...])
    width = pre.shape[1] // 2
    gate, up = pre[:, :width], pre[:, width:]
    sig = jax.nn.sigmoid(gate)
    d_hidden = times_transposed(cot, down[...])
    d_gate = d_hidden * up * sig * (1.0 + gate * (1.0 - sig))
    d_up = d_hidden * gate * sig
    both = jnp.concatenate([d_gate.astype(BF16), d_up.astype(BF16)], axis=1)
    return times_transposed(both, gate_up[...])


def loading_kernel(places, *refs):
    *parts, out_ref, sems = refs
    copies = []
    for number, (part, row) in enumerate(zip(parts, places, strict=True)):
        there = out_ref.at[pl.ds(row, part.shape[0]), pl.ds(0, part.shape[1])]
        copies.append(pltpu.make_async_copy(part, there, sems.at[number]))
        copies[-1].start()
    for copy in copies:
        copy.wait()


def loaded(arrays):
    places = [sum(array.shape[0] for array in arrays[:number]) for number in range(len(arrays))]
    shape = (sum(array.shape[0] for array in arrays), max(array.shape[1] for array in arrays))
    array = pl.pallas_call(
        functools.partial(loading_kernel, places),
        out_shape=jax.ShapeDtypeStruct(shape, arrays[0].dtype),
        in_specs=[pl.BlockSpec(memory_space=pl.ANY)] * len(arrays),
        out_specs=pl.BlockSpec(memory_space=pltpu.VMEM),
        scratch_shapes=[pltpu.SemaphoreType.DMA((len(arrays),))],
        compiler_params=pltpu.CompilerParams(vmem_limit_bytes=VMEM_LIMIT),
        cost_estimate=LITTLE,
    )(*arrays)
    return array, [(row, *part.shape) for row, part in zip(places, arrays, strict=True)]


def expert_kernel(each, topk, first, rows, step, copies, matrices, me_ref, *refs):
    count = 1 + max(operand for each_copy in copies for operand, *_ in each_copy)
    buffers, sems = refs[-1 - len(copies) : -1], refs[-1]
    out_refs = refs[count + 1 : -1 - len(copies)]
    weights = [refs[count].at[pl.ds(row, depth), pl.ds(0, across)] for row, depth, across in matrices]
    begins = [0]
    for pieces in copies:
        begins.append(begins[-1] + len(pieces))
    started = {}

    def start_copies(number):
        buffer, row = buffers[number], 0
        started[number] = []
        for piece, (operand, at, length, column) in enumerate(copies[number]):
            copy = pltpu.make_async_copy(
                refs[operand].at[pl.ds(at, length), pl.ds(column, buffer.shape[1])],
                buffer.at[pl.ds(row, length), :],
                sems.at[begins[number] + piece],
            )
            copy.start()
            started[number].append(copy)
            row += length

    def ready(number):
        for copy in started[number]:
            copy.wait()
        started[number] = []
        return buffers[number]

    inputs = len(copies) - 1
    for number in range(len(copies)):
        start_copies(number)
    total_rows = buffers[0].shape[0]
    places = [(out_ref, row) for out_ref in out_refs for row in range(0, out_ref.shape[0], rows)]
    totals = {}
    for flip in range(2):
        for start in range(0, total_rows, step * rows):
            tile = pl.ds(start, min(step * rows, total_rows - start))
            taken = [ready(number)[tile, :] for number in range(inputs)]
            gate_up, down = weights[2 * flip : 2 * flip + 2]
            out = each(*taken, gate_up, down).astype(BF16).astype(F32)
            out = out * gate_of(ready(len(copies) - 1)[tile, :], topk, first, me_ref[0] ^ flip)
            if flip == 0:
                totals[start] = out
                continue
            out = totals[start] + out
            for at in range(0, out.shape[0], rows):
                out_ref, row = places[(start + at) // rows]
                out_ref[pl.ds(row, rows), :] = out[at : at + rows].astype(out_ref.dtype)


def weighted(each, first, topk, rows, step, wanted, outputs, place, words, inputs, weights):
    weights, matrices = weights
    hidden_width, width = matrices[1][1:]
    operands, copies, scratch = [], [], []
    length = len(wanted) * rows

    def operand(array):
        for number, other in enumerate(operands):
            if other is array:
                return number
        operands.append(array)
        return len(operands) - 1

    def rows_from(parts, orders, columns, column):
        pieces = []
        for r in wanted:
            part, block = next((n, o.index(r)) for n, o in enumerate(orders) if r in o)
            number, at = operand(parts[part]), block * rows
            if pieces and pieces[-1][0] == number and pieces[-1][1] + pieces[-1][2] == at:
                pieces[-1] = (number, pieces[-1][1], pieces[-1][2] + rows, column)
            else:
                pieces.append((number, at, rows, column))
        copies.append(pieces)
        scratch.append(pltpu.VMEM((length, columns), BF16))

    for parts, orders in inputs:
        rows_from(parts, orders, width, 0)
    rows_from(*words, width)
    return pl.pallas_call(
        functools.partial(expert_kernel, each, topk, first, rows, step, copies, matrices),
        out_shape=[jax.ShapeDtypeStruct((number * rows, width), dtype) for number, dtype in outputs],
        in_specs=[pl.BlockSpec(memory_space=pltpu.SMEM)]
        + [pl.BlockSpec(memory_space=pl.ANY)] * len(operands)
        + [pl.BlockSpec(memory_space=pltpu.VMEM)],
        out_specs=[pl.BlockSpec(memory_space=pltpu.VMEM)] * len(outputs),
        scratch_shapes=scratch + [pltpu.SemaphoreType.DMA((sum(map(len, copies)),))],
        compiler_params=pltpu.CompilerParams(vmem_limit_bytes=VMEM_LIMIT),
        cost_estimate=pl.CostEstimate(
            flops=4 * (2 * len(inputs) + 1) * length * width * hidden_width,
            bytes_accessed=sum(a.size * a.dtype.itemsize for a in operands),
            transcendentals=0,
        ),
    )(place, *operands, weights)


def on_device(
    x_forward,
    route_forward,
    gate_forward,
    x_backward,
    route_backward,
    gate_backward,
    cotangent,
    w_gate,
    w_up,
    w_down,
):
    experts = lax.axis_size("expert")
    rows, width = x_forward.shape[1:]
    topk = route_forward.shape[2]
    me = lax.axis_index("expert").astype(jnp.int32)

    bits = []
    while 2 << len(bits) < experts:
        bits.insert(0, 2 << len(bits))
    blocks = experts // 2
    paths = (dict(zip(bits, bits)), dict(zip(bits, bits[:-2] + [bits[-1], bits[-2]])))
    back = bits[::-1]
    order = halving_order(back)

    arrays = {"f": x_forward[0], "b": x_backward[0], "c": cotangent[0]}
    words = [route_forward[0], gate_forward[0], route_backward[0], gate_backward[0]]
    held = {}

    arrays["f"] = packed(arrays["f"], *words)
    down0 = w_down[0, 0]
    pair = [w_gate[0, 0], w_up[0, 0]]
    *pair, down0 = behind([*pair, down0], [arrays["f"]])
    gate_up0 = jnp.concatenate(pair, axis=1)
    chip = [{1: 1}] * 2
    gate_up1, down1 = swapped(gate_up0, chip, 1), swapped(down0, chip, 1)
    weights = loaded([gate_up0, down0, gate_up1, down1])

    step = min(4, blocks // 2)
    place = jnp.reshape(me, (1,))

    far = passed_along(x_forward[0], 1, [{}, {}]), passed_along(cotangent[0], -1, [{}, {}])

    def arrived(rows_far, kind):
        one, other = held[kind].came[-2:]
        return (rows_far.astype(F32) + (one.astype(F32) + other.astype(F32))).astype(BF16)[None]

    outs = {}
    items = (TOGETHER if len(bits) < 4 else IN_TURN).split(",")
    left = {name: [item.split(":")[0] for item in items].count(name) for name in "fbcFB"}
    for item in items:
        name, _, after = item.partition(":")
        after = [outs[other] for other in after.split()]
        kind = name[0].lower()
        if len(name) == 1:
            if name not in held:
                held[name] = Spread(arrays[name], paths, bits)
            held[name].step(after)
            left[name] -= 1
            while left[name] == 0 and not held[name].done():
                held[name].step()
            continue
        takes = [(held[other].parts, held[other].orders) for other in ("f" if kind == "f" else "bc")]
        carrier = (held["f"].parts, held["f"].orders, held["f"].held.shape[1] - width)
        each, first = (forward_rows, 0) if kind == "f" else (backward_rows, 4)
        half = len(order) // 2
        wanted, results = {
            "s": (order[:half], [(half // 2, BF16)] * 2),
            "k": (order[half:], [(half, F32)]),
        }[name[1]]
        (place,) = behind([place], after)
        out = weighted(each, first, topk, rows, step, wanted, results, place, carrier, takes, weights)
        place, *out = lax.optimization_barrier((place, *out))
        outs[name] = out[0]
        if name[1] == "s":
            held[name[0]] = Return(out, paths, back, 1 if kind == "f" else -1)
        else:
            held[name[0]].keep = out[0]

    return arrived(far[0], "F"), arrived(far[1], "B")


def solution(mesh):
    in_specs = (
        P("section", "expert", None),
        P("section", "expert", None),
        P("section", "expert", None),
        P("section", "expert", None),
        P("section", "expert", None),
        P("section", "expert", None),
        P("section", "expert", None),
        P("section", "expert", None, None),
        P("section", "expert", None, None),
        P("section", "expert", None, None),
    )
    out_specs = (P("section", "expert", None), P("section", "expert", None))
    return jax.shard_map(
        on_device, mesh=mesh, in_specs=in_specs, out_specs=out_specs, check_vma=False
    )
```

```python
import functools

import jax
import jax.numpy as jnp
from jax import lax
from jax.experimental import pallas as pl
from jax.experimental.pallas import tpu as pltpu
from jax.sharding import PartitionSpec as P

F32 = jnp.float32
BF16 = jnp.bfloat16
LANES = 128
VMEM_LIMIT = 20 * 1024 * 1024
TOGETHER = "f,c,b,f,c,b,f,c,b,Fs,F,F,Fk,Bs,B,B,F,Bk,B,F,B"
IN_TURN = "f,Fs,F,Fk,F,b:Fk,c:Fk,Bs,B,Bk,B"
LITTLE = pl.CostEstimate(flops=1, bytes_accessed=1, transcendentals=0)


def passed_along(block, distance, paths, bit=0):
    sections, experts = lax.axis_size("section"), lax.axis_size("expert")
    route = [
        (s * experts + e, (s + distance) % sections * experts + (e ^ paths[e % 2].get(bit, 0)))
        for s in range(sections)
        for e in range(experts)
    ]
    return lax.ppermute(block, ("section", "expert"), route)


def swapped(block, paths, bit):
    route = [(i, i ^ paths[i % 2][bit]) for i in range(lax.axis_size("expert"))]
    return lax.ppermute(block, "expert", route)


class Spread:
    def __init__(self, block, paths, bits):
        self.paths, self.bits = paths, bits
        self.came, self.held, self.order = [], block, [0]

    def done(self):
        return len(self.came) == len(self.bits)

    def step(self, after=()):
        at = len(self.came)
        parts = behind([self.held] + self.came[-1:], after)
        self.held = parts[0] if at == 0 else jnp.concatenate(parts, axis=0)
        if at:
            self.order = self.order + [r | self.bits[at - 1] for r in self.order]
        self.came.append(swapped(self.held, self.paths, self.bits[at]))
        self.parts = [self.held, self.came[-1]]
        self.orders = [self.order, [r | self.bits[at] for r in self.order]]


def behind(arrays, others):
    if not others:
        return list(arrays)
    return list(lax.optimization_barrier((*arrays, *others))[: len(arrays)])


def halving_order(bits):
    order = [0]
    for bit in reversed(bits):
        order = [r | bit for r in order] + order
    return order


class Return:
    def __init__(self, sends, paths, bits, distance):
        self.sends, self.keep, self.came = sends, None, []
        self.paths, self.bits, self.distance = paths, bits, distance

    def done(self):
        return len(self.came) == len(self.bits) + 2

    def step(self, after=()):
        at = len(self.came)
        if at < 2:
            (send,) = behind([self.sends[at]], after)
            self.came.append(swapped(send, self.paths, self.bits[0]))
            return
        half = self.keep.shape[0] // 2
        if at == 2:
            send, self.keep = self.keep[:half] + self.came[0].astype(F32), self.keep[half:]
        else:
            total = self.keep + self.came[-1].astype(F32)
            if at == 3:
                total = total + self.came[1].astype(F32)
            half = total.shape[0] // 2
            send, self.keep = total[:half], total[half:]
        bit = self.bits[at - 1]
        if bit != self.bits[-1]:
            (send,) = behind([send.astype(BF16)], after)
            self.came.append(swapped(send, self.paths, bit))
        else:
            send, keep = behind([send.astype(BF16), self.keep.astype(BF16)], after)
            self.came.append(passed_along(keep, self.distance, self.paths))
            self.came.append(passed_along(send, self.distance, self.paths, bit))


def packing_kernel(x_ref, route_f, gate_f, route_b, gate_b, out_ref):
    width, extra = x_ref.shape[1], out_ref.shape[1] - x_ref.shape[1]
    out_ref[:, :width] = x_ref[...]
    pieces = []
    for route_ref, gate_ref in ((route_f, gate_f), (route_b, gate_b)):
        pieces.append(route_ref[...].astype(F32))
        rest = gate_ref[...]
        for _ in range(3):
            pieces.append(rest.astype(BF16).astype(F32))
            rest = rest - pieces[-1]
    used = sum(piece.shape[0] for piece in pieces)
    if extra > used:
        pieces.append(jnp.zeros((extra - used, x_ref.shape[0]), F32))
    out_ref[:, width:] = jnp.transpose(jnp.concatenate(pieces, axis=0)).astype(BF16)


def packed(rows, *words):
    length, width = rows.shape
    extra = 8 * words[0].shape[1]
    return pl.pallas_call(
        packing_kernel,
        out_shape=jax.ShapeDtypeStruct((length, width + extra + -extra % LANES), BF16),
        cost_estimate=LITTLE,
    )(rows, *[jnp.transpose(array) for array in words])


def gate_of(words, topk, first, expert):
    words = words.astype(F32)
    at = [words[:, (first + j) * topk : (first + j + 1) * topk] for j in range(4)]
    gates = at[1] + at[2] + at[3]
    chosen = at[0] == expert.astype(F32)
    return jnp.sum(jnp.where(chosen, gates, 0.0), axis=1, keepdims=True)


def times(a, b):
    return lax.dot_general(a, b, (((1,), (0,)), ((), ())), preferred_element_type=F32)


def times_transposed(a, b):
    return lax.dot_general(a, b, (((1,), (1,)), ((), ())), preferred_element_type=F32)


def forward_rows(x, gate_up, down):
    pre = times(x(), gate_up[...])
    width = pre.shape[1] // 2
    gate, up = pre[:, :width], pre[:, width:]
    hidden = (gate * jax.nn.sigmoid(gate) * up).astype(BF16)
    return times(hidden, down[...])


def backward_rows(x, cot, gate_up, down):
    pre = times(x(), gate_up[...])
    width = pre.shape[1] // 2
    gate, up = pre[:, :width], pre[:, width:]
    sig = jax.nn.sigmoid(gate)
    d_hidden = times_transposed(cot(), down[...])
    d_gate = d_hidden * up * sig * (1.0 + gate * (1.0 - sig))
    d_up = d_hidden * gate * sig
    both = jnp.concatenate([d_gate.astype(BF16), d_up.astype(BF16)], axis=1)
    return times_transposed(both, gate_up[...])


def loading_kernel(places, *refs):
    *parts, out_ref, sems = refs
    copies = []
    for number, (part, row) in enumerate(zip(parts, places, strict=True)):
        there = out_ref.at[pl.ds(row, part.shape[0]), pl.ds(0, part.shape[1])]
        copies.append(pltpu.make_async_copy(part, there, sems.at[number]))
        copies[-1].start()
    for copy in copies:
        copy.wait()


def loaded(arrays):
    places = [sum(array.shape[0] for array in arrays[:number]) for number in range(len(arrays))]
    shape = (sum(array.shape[0] for array in arrays), max(array.shape[1] for array in arrays))
    array = pl.pallas_call(
        functools.partial(loading_kernel, places),
        out_shape=jax.ShapeDtypeStruct(shape, arrays[0].dtype),
        in_specs=[pl.BlockSpec(memory_space=pl.ANY)] * len(arrays),
        out_specs=pl.BlockSpec(memory_space=pltpu.VMEM),
        scratch_shapes=[pltpu.SemaphoreType.DMA((len(arrays),))],
        compiler_params=pltpu.CompilerParams(vmem_limit_bytes=VMEM_LIMIT),
        cost_estimate=LITTLE,
    )(*arrays)
    return array, [(row, *part.shape) for row, part in zip(places, arrays, strict=True)]


def expert_kernel(each, topk, first, rows, step, copies, matrices, me_ref, *refs):
    count = 1 + max(operand for each_copy in copies for operand, *_ in each_copy)
    buffers, sems = refs[-1 - len(copies) : -1], refs[-1]
    out_refs = refs[count + 1 : -1 - len(copies)]
    weights = [refs[count].at[pl.ds(row, depth), pl.ds(0, across)] for row, depth, across in matrices]
    begins = [0]
    for pieces in copies:
        begins.append(begins[-1] + len(pieces))
    started = {}

    def start_copies(number):
        buffer, row = buffers[number], 0
        started[number] = []
        for piece, (operand, at, length, column) in enumerate(copies[number]):
            copy = pltpu.make_async_copy(
                refs[operand].at[pl.ds(at, length), pl.ds(column, buffer.shape[1])],
                buffer.at[pl.ds(row, length), :],
                sems.at[begins[number] + piece],
            )
            copy.start()
            started[number].append(copy)
            row += length

    def ready(number):
        for copy in started[number]:
            copy.wait()
        started[number] = []
        return buffers[number]

    def taken_rows(number, tile):
        return ready(number)[tile, :]

    inputs = len(copies) - 1
    for number in range(len(copies)):
        start_copies(number)
    total_rows = buffers[0].shape[0]
    places = [(out_ref, row) for out_ref in out_refs for row in range(0, out_ref.shape[0], rows)]
    totals = {}
    for flip in range(2):
        for start in range(0, total_rows, step * rows):
            tile = pl.ds(start, min(step * rows, total_rows - start))
            taken = [functools.partial(taken_rows, number, tile) for number in range(inputs)]
            gate_up, down = weights[2 * flip : 2 * flip + 2]
            out = each(*taken, gate_up, down).astype(BF16).astype(F32)
            out = out * gate_of(ready(len(copies) - 1)[tile, :], topk, first, me_ref[0] ^ flip)
            if flip == 0:
                totals[start] = out
                continue
            out = totals[start] + out
            for at in range(0, out.shape[0], rows):
                out_ref, row = places[(start + at) // rows]
                out_ref[pl.ds(row, rows), :] = out[at : at + rows].astype(out_ref.dtype)


def weighted(each, first, topk, rows, step, wanted, outputs, place, words, inputs, weights):
    weights, matrices = weights
    hidden_width, width = matrices[1][1:]
    operands, copies, scratch = [], [], []
    length = len(wanted) * rows

    def operand(array):
        for number, other in enumerate(operands):
            if other is array:
                return number
        operands.append(array)
        return len(operands) - 1

    def rows_from(parts, orders, columns, column):
        pieces = []
        for r in wanted:
            part, block = next((n, o.index(r)) for n, o in enumerate(orders) if r in o)
            number, at = operand(parts[part]), block * rows
            if pieces and pieces[-1][0] == number and pieces[-1][1] + pieces[-1][2] == at:
                pieces[-1] = (number, pieces[-1][1], pieces[-1][2] + rows, column)
            else:
                pieces.append((number, at, rows, column))
        copies.append(pieces)
        scratch.append(pltpu.VMEM((length, columns), BF16))

    for parts, orders in inputs:
        rows_from(parts, orders, width, 0)
    rows_from(*words, width)
    return pl.pallas_call(
        functools.partial(expert_kernel, each, topk, first, rows, step, copies, matrices),
        out_shape=[jax.ShapeDtypeStruct((number * rows, width), dtype) for number, dtype in outputs],
        in_specs=[pl.BlockSpec(memory_space=pltpu.SMEM)]
        + [pl.BlockSpec(memory_space=pl.ANY)] * len(operands)
        + [pl.BlockSpec(memory_space=pltpu.VMEM)],
        out_specs=[pl.BlockSpec(memory_space=pltpu.VMEM)] * len(outputs),
        scratch_shapes=scratch + [pltpu.SemaphoreType.DMA((sum(map(len, copies)),))],
        compiler_params=pltpu.CompilerParams(vmem_limit_bytes=VMEM_LIMIT),
        cost_estimate=pl.CostEstimate(
            flops=4 * (2 * len(inputs) + 1) * length * width * hidden_width,
            bytes_accessed=sum(a.size * a.dtype.itemsize for a in operands),
            transcendentals=0,
        ),
    )(place, *operands, weights)


def on_device(
    x_forward,
    route_forward,
    gate_forward,
    x_backward,
    route_backward,
    gate_backward,
    cotangent,
    w_gate,
    w_up,
    w_down,
):
    experts = lax.axis_size("expert")
    rows, width = x_forward.shape[1:]
    topk = route_forward.shape[2]
    me = lax.axis_index("expert").astype(jnp.int32)

    bits = []
    while 2 << len(bits) < experts:
        bits.insert(0, 2 << len(bits))
    blocks = experts // 2
    paths = (dict(zip(bits, bits)), dict(zip(bits, bits[:-2] + [bits[-1], bits[-2]])))
    back = bits[::-1]
    order = halving_order(back)

    arrays = {"f": x_forward[0], "b": x_backward[0], "c": cotangent[0]}
    words = [route_forward[0], gate_forward[0], route_backward[0], gate_backward[0]]
    held = {}

    arrays["f"] = packed(arrays["f"], *words)
    down0 = w_down[0, 0]
    pair = [w_gate[0, 0], w_up[0, 0]]
    *pair, down0 = behind([*pair, down0], [arrays["f"]])
    gate_up0 = jnp.concatenate(pair, axis=1)
    chip = [{1: 1}] * 2
    gate_up1, down1 = swapped(gate_up0, chip, 1), swapped(down0, chip, 1)
    weights = loaded([gate_up0, down0, gate_up1, down1])

    step = min(4, blocks // 2)
    place = jnp.reshape(me, (1,))

    far = passed_along(x_forward[0], 1, [{}, {}]), passed_along(cotangent[0], -1, [{}, {}])

    def arrived(rows_far, kind):
        one, other = held[kind].came[-2:]
        return (rows_far.astype(F32) + (one.astype(F32) + other.astype(F32))).astype(BF16)[None]

    outs = {}
    items = (TOGETHER if len(bits) < 4 else IN_TURN).split(",")
    left = {name: [item.split(":")[0] for item in items].count(name) for name in "fbcFB"}
    for item in items:
        name, _, after = item.partition(":")
        after = [outs[other] for other in after.split()]
        kind = name[0].lower()
        if len(name) == 1:
            if name not in held:
                held[name] = Spread(arrays[name], paths, bits)
            held[name].step(after)
            left[name] -= 1
            while left[name] == 0 and not held[name].done():
                held[name].step()
            continue
        takes = [(held[other].parts, held[other].orders) for other in ("f" if kind == "f" else "bc")]
        carrier = (held["f"].parts, held["f"].orders, held["f"].held.shape[1] - width)
        each, first = (forward_rows, 0) if kind == "f" else (backward_rows, 4)
        half = len(order) // 2
        wanted, results = {
            "s": (order[:half], [(half // 2, BF16)] * 2),
            "k": (order[half:], [(half, F32)]),
        }[name[1]]
        (place,) = behind([place], after)
        out = weighted(each, first, topk, rows, step, wanted, results, place, carrier, takes, weights)
        place, *out = lax.optimization_barrier((place, *out))
        outs[name] = out[0]
        if name[1] == "s":
            held[name[0]] = Return(out, paths, back, 1 if kind == "f" else -1)
        else:
            held[name[0]].keep = out[0]

    return arrived(far[0], "F"), arrived(far[1], "B")


def solution(mesh):
    in_specs = (
        P("section", "expert", None),
        P("section", "expert", None),
        P("section", "expert", None),
        P("section", "expert", None),
        P("section", "expert", None),
        P("section", "expert", None),
        P("section", "expert", None),
        P("section", "expert", None, None),
        P("section", "expert", None, None),
        P("section", "expert", None, None),
    )
    out_specs = (P("section", "expert", None), P("section", "expert", None))
    return jax.shard_map(
        on_device, mesh=mesh, in_specs=in_specs, out_specs=out_specs, check_vma=False
    )
```

```python
import functools

import jax
import jax.numpy as jnp
from jax import lax
from jax.experimental import pallas as pl
from jax.experimental.pallas import tpu as pltpu
from jax.sharding import PartitionSpec as P

F32 = jnp.float32
BF16 = jnp.bfloat16
LANES = 128
VMEM_LIMIT = 20 * 1024 * 1024
TOGETHER = "f,c,b,f,c,b,f,c,b,Fs,F,F,Fk,Bs,B,B,F,Bk,B,F,B"
IN_TURN = "f,Fs,F,Fk,F,b:Fk,c:Fk,Bs,B,Bk,B"
LITTLE = pl.CostEstimate(flops=1, bytes_accessed=1, transcendentals=0)


def passed_along(block, distance, paths, bit=0):
    sections, experts = lax.axis_size("section"), lax.axis_size("expert")
    route = [
        (s * experts + e, (s + distance) % sections * experts + (e ^ paths[e % 2].get(bit, 0)))
        for s in range(sections)
        for e in range(experts)
    ]
    return lax.ppermute(block, ("section", "expert"), route)


def swapped(block, paths, bit):
    route = [(i, i ^ paths[i % 2][bit]) for i in range(lax.axis_size("expert"))]
    return lax.ppermute(block, "expert", route)


class Spread:
    def __init__(self, block, paths, bits):
        self.paths, self.bits = paths, bits
        self.came, self.held, self.order = [], block, [0]

    def done(self):
        return len(self.came) == len(self.bits)

    def step(self, after=()):
        at = len(self.came)
        parts = behind([self.held] + self.came[-1:], after)
        self.held = parts[0] if at == 0 else jnp.concatenate(parts, axis=0)
        if at:
            self.order = self.order + [r | self.bits[at - 1] for r in self.order]
        self.came.append(swapped(self.held, self.paths, self.bits[at]))
        self.parts = [self.held, self.came[-1]]
        self.orders = [self.order, [r | self.bits[at] for r in self.order]]


def behind(arrays, others):
    if not others:
        return list(arrays)
    return list(lax.optimization_barrier((*arrays, *others))[: len(arrays)])


def halving_order(bits):
    order = [0]
    for bit in reversed(bits):
        order = [r | bit for r in order] + order
    return order


class Return:
    def __init__(self, sends, paths, bits, distance):
        self.sends, self.keep, self.came = sends, None, []
        self.paths, self.bits, self.distance = paths, bits, distance

    def done(self):
        return len(self.came) == len(self.bits) + 2

    def step(self, after=()):
        at = len(self.came)
        if at < 2:
            (send,) = behind([self.sends[at]], after)
            self.came.append(swapped(send, self.paths, self.bits[0]))
            return
        half = self.keep.shape[0] // 2
        if at == 2:
            send, self.keep = self.keep[:half] + self.came[0].astype(F32), self.keep[half:]
        else:
            total = self.keep + self.came[-1].astype(F32)
            if at == 3:
                total = total + self.came[1].astype(F32)
            half = total.shape[0] // 2
            send, self.keep = total[:half], total[half:]
        bit = self.bits[at - 1]
        if bit != self.bits[-1]:
            (send,) = behind([send.astype(BF16)], after)
            self.came.append(swapped(send, self.paths, bit))
        else:
            send, keep = behind([send.astype(BF16), self.keep.astype(BF16)], after)
            self.came.append(passed_along(keep, self.distance, self.paths))
            self.came.append(passed_along(send, self.distance, self.paths, bit))


def packing_kernel(x_ref, route_f, gate_f, route_b, gate_b, out_ref):
    width, extra = x_ref.shape[1], out_ref.shape[1] - x_ref.shape[1]
    out_ref[:, :width] = x_ref[...]
    pieces = []
    for route_ref, gate_ref in ((route_f, gate_f), (route_b, gate_b)):
        pieces.append(route_ref[...].astype(F32))
        rest = gate_ref[...]
        for _ in range(3):
            pieces.append(rest.astype(BF16).astype(F32))
            rest = rest - pieces[-1]
    used = sum(piece.shape[0] for piece in pieces)
    if extra > used:
        pieces.append(jnp.zeros((extra - used, x_ref.shape[0]), F32))
    out_ref[:, width:] = jnp.transpose(jnp.concatenate(pieces, axis=0)).astype(BF16)


def packed(rows, *words):
    length, width = rows.shape
    extra = 8 * words[0].shape[1]
    return pl.pallas_call(
        packing_kernel,
        out_shape=jax.ShapeDtypeStruct((length, width + extra + -extra % LANES), BF16),
        cost_estimate=LITTLE,
    )(rows, *[jnp.transpose(array) for array in words])


def gate_of(words, topk, first, expert):
    words = words.astype(F32)
    at = [words[:, (first + j) * topk : (first + j + 1) * topk] for j in range(4)]
    gates = at[1] + at[2] + at[3]
    chosen = at[0] == expert.astype(F32)
    return jnp.sum(jnp.where(chosen, gates, 0.0), axis=1, keepdims=True)


def times(a, b):
    return lax.dot_general(a, b, (((1,), (0,)), ((), ())), preferred_element_type=F32)


def times_transposed(a, b):
    return lax.dot_general(a, b, (((1,), (1,)), ((), ())), preferred_element_type=F32)


def forward_rows(x, gate_up, down):
    pre = times(x, gate_up[...])
    width = pre.shape[1] // 2
    gate, up = pre[:, :width], pre[:, width:]
    hidden = (gate * jax.nn.sigmoid(gate) * up).astype(BF16)
    return times(hidden, down[...])


def backward_rows(x, cot, gate_up, down):
    pre = times(x, gate_up[...])
    width = pre.shape[1] // 2
    gate, up = pre[:, :width], pre[:, width:]
    sig = jax.nn.sigmoid(gate)
    d_hidden = times_transposed(cot, down[...])
    d_gate = d_hidden * up * sig * (1.0 + gate * (1.0 - sig))
    d_up = d_hidden * gate * sig
    both = jnp.concatenate([d_gate.astype(BF16), d_up.astype(BF16)], axis=1)
    return times_transposed(both, gate_up[...])


def loading_kernel(places, *refs):
    *parts, out_ref, sems = refs
    copies = []
    for number, (part, row) in enumerate(zip(parts, places, strict=True)):
        there = out_ref.at[pl.ds(row, part.shape[0]), pl.ds(0, part.shape[1])]
        copies.append(pltpu.make_async_copy(part, there, sems.at[number]))
        copies[-1].start()
    for copy in copies:
        copy.wait()


def loaded(arrays):
    places = [sum(array.shape[0] for array in arrays[:number]) for number in range(len(arrays))]
    shape = (sum(array.shape[0] for array in arrays), max(array.shape[1] for array in arrays))
    array = pl.pallas_call(
        functools.partial(loading_kernel, places),
        out_shape=jax.ShapeDtypeStruct(shape, arrays[0].dtype),
        in_specs=[pl.BlockSpec(memory_space=pl.ANY)] * len(arrays),
        out_specs=pl.BlockSpec(memory_space=pltpu.VMEM),
        scratch_shapes=[pltpu.SemaphoreType.DMA((len(arrays),))],
        compiler_params=pltpu.CompilerParams(vmem_limit_bytes=VMEM_LIMIT),
        cost_estimate=LITTLE,
    )(*arrays)
    return array, [(row, *part.shape) for row, part in zip(places, arrays, strict=True)]


def expert_kernel(each, topk, first, rows, step, copies, matrices, me_ref, *refs):
    count = 1 + max(operand for each_copy in copies for operand, *_ in each_copy)
    buffers, sems = refs[-1 - len(copies) : -1], refs[-1]
    out_refs = refs[count + 1 : -1 - len(copies)]
    weights = [refs[count].at[pl.ds(row, depth), pl.ds(0, across)] for row, depth, across in matrices]
    begins = [0]
    for pieces in copies:
        begins.append(begins[-1] + len(pieces))
    started = {}

    def start_copies(number):
        buffer, row = buffers[number], 0
        started[number] = []
        for piece, (operand, at, length, column) in enumerate(copies[number]):
            copy = pltpu.make_async_copy(
                refs[operand].at[pl.ds(at, length), pl.ds(column, buffer.shape[1])],
                buffer.at[pl.ds(row, length), :],
                sems.at[begins[number] + piece],
            )
            copy.start()
            started[number].append(copy)
            row += length

    def ready(number):
        for copy in started[number]:
            copy.wait()
        started[number] = []
        return buffers[number]

    inputs = len(copies) - 1
    for number in range(len(copies)):
        start_copies(number)
    total_rows = buffers[0].shape[0]
    places = [(out_ref, row) for out_ref in out_refs for row in range(0, out_ref.shape[0], rows)]
    totals = {}
    for flip in range(2):
        for start in range(0, total_rows, step * rows):
            tile = pl.ds(start, min(step * rows, total_rows - start))
            taken = [ready(number)[tile, :] for number in range(inputs)]
            gate_up, down = weights[2 * flip : 2 * flip + 2]
            out = each(*taken, gate_up, down).astype(BF16).astype(F32)
            out = out * gate_of(ready(len(copies) - 1)[tile, :], topk, first, me_ref[0] ^ flip)
            if flip == 0:
                totals[start] = out
                continue
            out = totals[start] + out
            for at in range(0, out.shape[0], rows):
                out_ref, row = places[(start + at) // rows]
                out_ref[pl.ds(row, rows), :] = out[at : at + rows].astype(out_ref.dtype)


def weighted(each, first, topk, rows, step, wanted, outputs, place, words, inputs, weights):
    weights, matrices = weights
    hidden_width, width = matrices[1][1:]
    operands, copies, scratch = [], [], []
    length = len(wanted) * rows

    def operand(array):
        for number, other in enumerate(operands):
            if other is array:
                return number
        operands.append(array)
        return len(operands) - 1

    def rows_from(parts, orders, columns, column):
        pieces = []
        for r in wanted:
            part, block = next((n, o.index(r)) for n, o in enumerate(orders) if r in o)
            number, at = operand(parts[part]), block * rows
            if pieces and pieces[-1][0] == number and pieces[-1][1] + pieces[-1][2] == at:
                pieces[-1] = (number, pieces[-1][1], pieces[-1][2] + rows, column)
            else:
                pieces.append((number, at, rows, column))
        copies.append(pieces)
        scratch.append(pltpu.VMEM((length, columns), BF16))

    for parts, orders in inputs:
        rows_from(parts, orders, width, 0)
    rows_from(*words, width)
    return pl.pallas_call(
        functools.partial(expert_kernel, each, topk, first, rows, step, copies, matrices),
        out_shape=[jax.ShapeDtypeStruct((number * rows, width), dtype) for number, dtype in outputs],
        in_specs=[pl.BlockSpec(memory_space=pltpu.SMEM)]
        + [pl.BlockSpec(memory_space=pl.ANY)] * len(operands)
        + [pl.BlockSpec(memory_space=pltpu.VMEM)],
        out_specs=[pl.BlockSpec(memory_space=pltpu.VMEM)] * len(outputs),
        scratch_shapes=scratch + [pltpu.SemaphoreType.DMA((sum(map(len, copies)),))],
        compiler_params=pltpu.CompilerParams(vmem_limit_bytes=VMEM_LIMIT),
        cost_estimate=pl.CostEstimate(
            flops=4 * (2 * len(inputs) + 1) * length * width * hidden_width,
            bytes_accessed=sum(a.size * a.dtype.itemsize for a in operands),
            transcendentals=0,
        ),
    )(place, *operands, weights)


def on_device(
    x_forward,
    route_forward,
    gate_forward,
    x_backward,
    route_backward,
    gate_backward,
    cotangent,
    w_gate,
    w_up,
    w_down,
):
    experts = lax.axis_size("expert")
    rows, width = x_forward.shape[1:]
    topk = route_forward.shape[2]
    me = lax.axis_index("expert").astype(jnp.int32)

    bits = []
    while 2 << len(bits) < experts:
        bits.insert(0, 2 << len(bits))
    blocks = experts // 2
    paths = (dict(zip(bits, bits)), dict(zip(bits, bits[:-2] + [bits[-1], bits[-2]])))
    back = bits[::-1]
    order = halving_order(back)

    arrays = {"f": x_forward[0], "b": x_backward[0], "c": cotangent[0]}
    words = [route_forward[0], gate_forward[0], route_backward[0], gate_backward[0]]
    held = {}

    arrays["f"] = packed(arrays["f"], *words)
    down0 = w_down[0, 0]
    pair = [w_gate[0, 0], w_up[0, 0]]
    pair = behind(pair, [arrays["f"]])
    gate_up0 = jnp.concatenate(pair, axis=1)
    chip = [{1: 1}] * 2
    gate_up1, down1 = swapped(gate_up0, chip, 1), swapped(down0, chip, 1)
    weights = loaded([gate_up0, down0, gate_up1, down1])

    step = min(4, blocks // 2)
    place = jnp.reshape(me, (1,))

    far = passed_along(x_forward[0], 1, [{}, {}]), passed_along(cotangent[0], -1, [{}, {}])

    def arrived(rows_far, kind):
        one, other = held[kind].came[-2:]
        return (rows_far.astype(F32) + (one.astype(F32) + other.astype(F32))).astype(BF16)[None]

    outs = {}
    items = (TOGETHER if len(bits) < 4 else IN_TURN).split(",")
    left = {name: [item.split(":")[0] for item in items].count(name) for name in "fbcFB"}
    for item in items:
        name, _, after = item.partition(":")
        after = [outs[other] for other in after.split()]
        kind = name[0].lower()
        if len(name) == 1:
            if name not in held:
                held[name] = Spread(arrays[name], paths, bits)
            held[name].step(after)
            left[name] -= 1
            while left[name] == 0 and not held[name].done():
                held[name].step()
            continue
        takes = [(held[other].parts, held[other].orders) for other in ("f" if kind == "f" else "bc")]
        carrier = (held["f"].parts, held["f"].orders, held["f"].held.shape[1] - width)
        each, first = (forward_rows, 0) if kind == "f" else (backward_rows, 4)
        half = len(order) // 2
        wanted, results = {
            "s": (order[:half], [(half // 2, BF16)] * 2),
            "k": (order[half:], [(half, F32)]),
        }[name[1]]
        (place,) = behind([place], after)
        out = weighted(each, first, topk, rows, step, wanted, results, place, carrier, takes, weights)
        place, *out = lax.optimization_barrier((place, *out))
        outs[name] = out[0]
        if name[1] == "s":
            held[name[0]] = Return(out, paths, back, 1 if kind == "f" else -1)
        else:
            held[name[0]].keep = out[0]

    return arrived(far[0], "F"), arrived(far[1], "B")


def solution(mesh):
    in_specs = (
        P("section", "expert", None),
        P("section", "expert", None),
        P("section", "expert", None),
        P("section", "expert", None),
        P("section", "expert", None),
        P("section", "expert", None),
        P("section", "expert", None),
        P("section", "expert", None, None),
        P("section", "expert", None, None),
        P("section", "expert", None, None),
    )
    out_specs = (P("section", "expert", None), P("section", "expert", None))
    return jax.shard_map(
        on_device, mesh=mesh, in_specs=in_specs, out_specs=out_specs, check_vma=False
    )
```
